512 devices in a mesh: fsdp: 32 (over z, core), expert: 16 (over x, y).
Axes of the slice: x: 4, y: 4, z: 16, core: 2. Of those that a mesh axis runs over, the one named last changes fastest.
Arguments:
- tokens: bfloat16 [65536, 4096], P(('fsdp', 'expert')), may hold values from -6 to 6
- expert_ids: int32 [65536, 2], P(('fsdp', 'expert')), may hold values from 0 to 15, all different within a row
- gate_probs: float32 [65536, 2], P(('fsdp', 'expert')), may hold values from 0.1 to 1
- up_weight: bfloat16 [16, 4096, 768], P('expert', 'fsdp'), may hold values from -0.09375 to 0.09375
- down_weight: bfloat16 [16, 768, 4096], P('expert', None, 'fsdp'), may hold values from -0.21875 to 0.21875
- out_grad: bfloat16 [65536, 4096], P(('fsdp', 'expert')), may hold values from -6 to 6
Outputs:
- d_tokens: bfloat16 [65536, 4096], P(('fsdp', 'expert'))
- d_gates: bfloat16 [65536, 2], P(('fsdp', 'expert'))
The draws below stay inside these ranges and needn't reach their ends.
Inputs may be any that keep to these rules, and one draw needn't show every extreme that they name: `expert_ids`: each token names two different experts, and every expert is named by some token.
All inputs are finite; a program needn't handle non-finite values.
Results may differ from the reference program's by a relative error of at most 0.017.
Values may be sent and summed in bfloat16 or wider, within the bound.
No kernel may reach another device: no remote copies, remote signals or barrier semaphores. Data moves between devices by JAX's collectives and lax.ppermute only.
A program may use at most 64 MiB of HBM per device.

```python
import jax
import jax.numpy as jnp
from jax import lax

D = 4096
FF = 768
TOK_DEV = 128
EXPERTS = 16
CAP = 12
TOKENS = 65536


def block_scale(stream_key, extent, cuts, smallest, high):
    def one(dim, shards_of):
        heights = jax.random.uniform(jax.random.fold_in(jax.random.fold_in(stream_key, 6), dim), (shards_of,), jnp.float32, smallest / len(cuts), high / len(cuts))
        return jnp.repeat(jnp.exp(heights), extent[dim] // shards_of).reshape((-1,) + (1,) * (len(extent) - dim - 1))

    factor_of = one(*cuts[0])
    for cut in cuts[1:]:
        factor_of = factor_of * one(*cut)
    return factor_of


def distinct(stream_key, rows, number_of, top, lift):
    sequence = jax.random.permutation(jax.random.fold_in(stream_key, 1), number_of)
    favour = sequence
    for power in range(3):
        favour = favour * favour // number_of
    favour = favour * lift // number_of
    chance = jax.random.randint(jax.random.fold_in(stream_key, 2), (rows, number_of), 0, 4096) + favour
    holders = jax.random.permutation(jax.random.fold_in(stream_key, 3), rows)[jnp.arange(number_of) % rows]
    chance = jnp.where(jnp.arange(rows)[:, None] == holders[None, :], 1 << 14, chance)
    merit = chance * number_of + jnp.arange(number_of)
    return lax.top_k(merit.astype(jnp.int32), top)[1].astype(jnp.int32)


def bell_draw(stream_key, shape, scale, bound, split=(), held_as=jnp.bfloat16):
    entries = jax.random.normal(stream_key, shape, jnp.float32) * scale
    if len(split) > 0:
        entries = block_scale(stream_key, shape, split, -0.22, 0.18) * entries
    return jnp.clip(entries, min=-bound, max=bound).astype(held_as)


def setup_inputs(seed: int = 0) -> dict:
    key_of = jax.random.split(jax.random.key(seed), 7)
    tokens = bell_draw(key_of[0], (TOKENS, D), 1.0, 6.0, ((0, 512),))
    expert_ids = distinct(key_of[1], TOKENS, EXPERTS, 2, 1024)
    gate_probs = jnp.clip(0.1 + 0.9 * jax.random.uniform(key_of[2], (TOKENS, 2), jnp.float32) ** block_scale(key_of[2], (TOKENS, 2), ((0, 512),), -0.2, 0.2), 0.1, 1.0)
    up_weight = bell_draw(key_of[3], (EXPERTS, D, FF), D ** -0.5, 0.09375, ((0, 16), (1, 32)))
    down_weight = bell_draw(key_of[4], (EXPERTS, FF, D), FF ** -0.5, 0.21875, ((0, 16), (2, 32)))
    out_grad = bell_draw(key_of[5], (TOKENS, D), 1.0, 6.0, ((0, 512),))
    return dict(tokens=tokens, expert_ids=expert_ids, gate_probs=gate_probs, up_weight=up_weight, down_weight=down_weight, out_grad=out_grad)


def gelu_parts(hidden):
    normal_cdf = 0.5 * (1.0 + lax.erf(hidden * 0.7071067811865476))
    density = jnp.exp(-0.5 * hidden * hidden) * 0.3989422804014327
    return hidden * normal_cdf, normal_cdf + hidden * density


def expert_rows(row_tokens, row_grads, up_full, down_full):
    hidden = jnp.dot(row_tokens, up_full, preferred_element_type=jnp.float32)
    value, slope = gelu_parts(hidden)
    active = value.astype(jnp.bfloat16)
    active_grad = jnp.dot(row_grads, down_full.T, preferred_element_type=jnp.float32)
    gate_grad = jnp.sum(active.astype(jnp.float32) * active_grad, axis=1).astype(jnp.bfloat16)
    hidden_grad = (active_grad * slope).astype(jnp.bfloat16)
    input_grad = jnp.dot(hidden_grad, up_full.T, preferred_element_type=jnp.float32).astype(jnp.bfloat16)
    return input_grad, gate_grad


def reference(tokens, expert_ids, gate_probs, up_weight, down_weight, out_grad):
    blocks = TOKENS // TOK_DEV
    count_all = EXPERTS * CAP
    flat_ids = expert_ids.reshape(blocks, 2 * TOK_DEV).astype(jnp.int32)
    onehot = (flat_ids[:, :, None] == jnp.arange(EXPERTS, dtype=jnp.int32)[None, None, :]).astype(jnp.int32)
    position = jnp.sum((jnp.cumsum(onehot, axis=1) - 1) * onehot, axis=2).astype(jnp.int32)
    kept_mask = position < CAP
    clipped = jnp.minimum(position, CAP - 1).astype(jnp.int32)
    target = jnp.where(kept_mask, flat_ids * CAP + clipped, count_all).astype(jnp.int32)
    block_index = jnp.broadcast_to(jnp.arange(blocks, dtype=jnp.int32)[:, None], flat_ids.shape)
    owners = jnp.broadcast_to((jnp.arange(2 * TOK_DEV, dtype=jnp.int32) // 2)[None, :], flat_ids.shape)
    table = jnp.full((blocks, count_all), -1, jnp.int32)
    table = table.at[block_index, target].set(owners, mode="drop")
    filled = table >= 0
    source = jnp.maximum(table, 0).astype(jnp.int32)
    token_blocks = tokens.reshape(blocks, TOK_DEV, D)
    grad_blocks = out_grad.reshape(blocks, TOK_DEV, D)

    def one_expert(expert):
        start = (expert * CAP).astype(jnp.int32)
        rows = lax.dynamic_slice_in_dim(source, start, CAP, 1)
        live = lax.dynamic_slice_in_dim(filled, start, CAP, 1)[:, :, None]
        row_tokens = jnp.where(live, jnp.take_along_axis(token_blocks, rows[:, :, None], axis=1), 0).astype(jnp.bfloat16)
        row_grads = jnp.where(live, jnp.take_along_axis(grad_blocks, rows[:, :, None], axis=1), 0).astype(jnp.bfloat16)
        up_full = lax.dynamic_index_in_dim(up_weight, expert, 0, keepdims=False)
        down_full = lax.dynamic_index_in_dim(down_weight, expert, 0, keepdims=False)
        input_grad, gate_grad = expert_rows(row_tokens.reshape(blocks * CAP, D), row_grads.reshape(blocks * CAP, D), up_full, down_full)
        return input_grad.reshape(blocks, CAP, D), gate_grad.reshape(blocks, CAP)

    all_inputs, all_gates = lax.map(one_expert, jnp.arange(EXPERTS, dtype=jnp.int32))
    weight = jnp.where(kept_mask, gate_probs.reshape(blocks, 2 * TOK_DEV), 0.0).astype(jnp.float32)
    ids_pair = flat_ids.reshape(blocks, TOK_DEV, 2)
    pos_pair = clipped.reshape(blocks, TOK_DEV, 2)
    weight_pair = weight.reshape(blocks, TOK_DEV, 2)
    rows_index = jnp.broadcast_to(jnp.arange(blocks, dtype=jnp.int32)[:, None], (blocks, TOK_DEV))
    total = jnp.zeros((blocks, TOK_DEV, D), jnp.float32)
    for choice_k in range(2):
        picked = all_inputs[ids_pair[:, :, choice_k], rows_index, pos_pair[:, :, choice_k]]
        total = total + picked.astype(jnp.float32) * weight_pair[:, :, choice_k][:, :, None]
    d_tokens = total.astype(jnp.bfloat16).reshape(TOKENS, D)
    gate_picked = all_gates[flat_ids, block_index, clipped]
    d_gates = jnp.where(kept_mask, gate_picked, 0).astype(jnp.bfloat16).reshape(TOKENS, 2)
    return d_tokens, d_gates
```

```python
import functools

import jax
import jax.numpy as jnp
from jax import lax
from jax.experimental import pallas as pl
from jax.experimental.pallas import tpu as pltpu
from jax.sharding import PartitionSpec as P

F32, BF16 = jnp.float32, jnp.bfloat16
VMEM_LIMIT = 56 * 1024 * 1024


def dot(left, right):
    return jnp.dot(left, right, preferred_element_type=F32)


def dot_t(left, right):
    return lax.dot_general(left, right, (((1,), (1,)), ((), ())), preferred_element_type=F32)


def iota(shape, axis):
    return lax.broadcasted_iota(jnp.int32, shape, axis)


def params(*semantics):
    return pltpu.CompilerParams(dimension_semantics=semantics, vmem_limit_bytes=VMEM_LIMIT)


def slot_table(ids, experts, capacity):
    tokens = ids.shape[1]
    expert = iota((experts, tokens), 0)
    named = (expert == ids[0:1, :]) | (expert == ids[1:2, :])
    before = (iota((tokens, tokens), 0) < iota((tokens, tokens), 1)).astype(F32).astype(BF16)
    count = dot(named.astype(F32).astype(BF16), before)
    return jnp.where(named & (count < capacity), count, -1.0)


def dispatch_kernel(experts, capacity, ids_ref, gates_ref, tl, th, gl, gh, send_ref, mix_ref, own_ref, pick):
    rows = 2 * capacity
    tokens = ids_ref.shape[1]

    @pl.when(pl.program_id(0) == 0)
    def _():
        ids = ids_ref[...]
        table = slot_table(ids, experts, capacity)
        count = experts * rows
        spread = (iota((count, experts), 0) // rows == iota((count, experts), 1)).astype(F32).astype(BF16)
        place = iota((count, tokens), 0) % rows
        slot = dot(spread, table.astype(BF16)).astype(jnp.int32)
        low = slot == place
        high = (slot >= 0) & (slot + capacity == place)
        pick[0] = low.astype(F32).astype(BF16)
        pick[1] = high.astype(F32).astype(BF16)
        expert = iota((experts, tokens), 0)
        gates = gates_ref[...]
        weight = jnp.where(expert == ids[0:1, :], gates[0:1, :], gates[1:2, :])
        coarse = weight.astype(BF16)
        fine = (weight - coarse.astype(F32)).astype(BF16)
        for part, value in enumerate((coarse, fine)):
            wide = dot(spread, value)
            for half, chosen in enumerate((low, high)):
                mix_ref[half, part] = jnp.where(chosen, wide, 0.0).T.astype(BF16)
        whose = iota((count, tokens), 0) // rows
        for choice in range(2):
            own_ref[choice] = (low & (whose == ids[choice : choice + 1, :])).astype(F32).astype(BF16)

    count = experts * rows
    width = send_ref.shape[2]
    for part, (left, right) in enumerate(((tl, th), (gl, gh))):
        moved = dot(pick[0], left[...]) + dot(pick[1], right[...])
        send_ref[:, part * rows : (part + 1) * rows, :] = moved.astype(BF16).reshape(experts, rows, width)


def dispatch(ids, gates, tokens, grads, experts, capacity):
    count, width = tokens.shape
    rows = 2 * capacity
    blocks, block = 4, width // 8
    low = pl.BlockSpec((count, block), lambda i: (0, i))
    high = pl.BlockSpec((count, block), lambda i: (0, i + blocks))
    whole = lambda shape: pl.BlockSpec(shape, lambda i: (0,) * len(shape))
    return pl.pallas_call(
        functools.partial(dispatch_kernel, experts, capacity),
        grid=(blocks,),
        in_specs=[whole(ids.shape), whole(gates.shape), low, high, low, high],
        out_specs=[
            pl.BlockSpec((experts, 2 * rows, block), lambda i: (0, 0, i)),
            whole((2, 2, count, experts * rows)),
            whole((2, experts * rows, count)),
        ],
        out_shape=[
            jax.ShapeDtypeStruct((experts, 2 * rows, width // 2), BF16),
            jax.ShapeDtypeStruct((2, 2, count, experts * rows), BF16),
            jax.ShapeDtypeStruct((2, experts * rows, count), BF16),
        ],
        scratch_shapes=[pltpu.VMEM((2, experts * rows, count), BF16)],
        compiler_params=params("arbitrary"),
        name="dispatch",
    )(ids, gates, tokens, tokens, grads, grads)


def unpack_kernel(capacity, recv_ref, tokens_ref, grads_ref):
    slots = tokens_ref.shape[0]
    total = recv_ref.shape[0]
    row, column = iota((slots, total), 0), iota((slots, total), 1)
    base = (row // capacity) * (4 * capacity) + row % capacity
    half = pl.program_id(0) % 2
    for part, out in enumerate((tokens_ref, grads_ref)):
        take = column == base + (2 * part + half) * capacity
        out[...] = dot(take.astype(F32).astype(BF16), recv_ref[...]).astype(BF16)


def unpack(recv, capacity):
    total, half_width = recv.shape
    slots = total // 4
    blocks = 2
    block = half_width // blocks
    out = pl.BlockSpec((slots, block), lambda i: (0, (i % 2) * blocks + i // 2))
    return pl.pallas_call(
        functools.partial(unpack_kernel, capacity),
        grid=(2 * blocks,),
        in_specs=[pl.BlockSpec((total, block), lambda i: (0, i // 2))],
        out_specs=[out, out],
        out_shape=[jax.ShapeDtypeStruct((slots, 2 * half_width), BF16)] * 2,
        compiler_params=params("arbitrary"),
        name="unpack",
    )(recv)


def expert_kernel(capacity, blocks, x_ref, g_ref, w_ref, out_ref, up, hidden, active_grad):
    step = pl.program_id(0)
    slots, hidden_width = hidden.shape
    part_hidden = dot(x_ref[...], w_ref[:, :hidden_width])
    part_grad = dot(g_ref[...], w_ref[:, hidden_width:])
    up[step] = w_ref[:, :hidden_width]

    @pl.when(step == 0)
    def _():
        hidden[...] = part_hidden
        active_grad[...] = part_grad

    @pl.when(step > 0)
    def _():
        hidden[...] += part_hidden
        active_grad[...] += part_grad

    @pl.when(step == blocks - 1)
    def _():
        h = hidden[...]
        a = active_grad[...]
        cdf = 0.5 * (1.0 + lax.erf(h * 0.7071067811865476))
        density = jnp.exp(-0.5 * h * h) * 0.3989422804014327
        active = (h * cdf).astype(BF16).astype(F32)
        gate = jnp.sum(active * a, axis=1, keepdims=True).astype(BF16)
        hidden_grad = (a * (cdf + h * density)).astype(BF16)
        rows = 2 * capacity
        total = 2 * slots
        row, column = iota((total, slots), 0), iota((total, slots), 1)
        base = (row // rows) * capacity + row % rows
        low = (column == base) & (row % rows < capacity)
        high = (column == base - capacity) & (row % rows >= capacity)
        low, high = low.astype(F32).astype(BF16), high.astype(F32).astype(BF16)
        block = up.shape[1]
        for i in range(blocks // 2):
            left = dot_t(hidden_grad, up[i]).astype(BF16)
            right = dot_t(hidden_grad, up[i + blocks // 2]).astype(BF16)
            out_ref[:, i * block : (i + 1) * block] = (dot(low, left) + dot(high, right)).astype(BF16)
        lanes = jnp.broadcast_to(gate, (slots, 128))
        out_ref[:, blocks // 2 * block :] = dot(low, lanes).astype(BF16)


def expert(x, g, weights, capacity):
    slots, width = x.shape
    wide = weights.shape[1]
    blocks = 8
    block = width // blocks
    columns = pl.BlockSpec((slots, block), lambda i: (0, i))
    return pl.pallas_call(
        functools.partial(expert_kernel, capacity, blocks),
        grid=(blocks,),
        in_specs=[columns, columns, pl.BlockSpec((block, wide), lambda i: (i, 0))],
        out_specs=pl.BlockSpec((2 * slots, width // 2 + 128), lambda i: (0, 0)),
        out_shape=jax.ShapeDtypeStruct((2 * slots, width // 2 + 128), BF16),
        scratch_shapes=[
            pltpu.VMEM((blocks, block, wide // 2), BF16),
            pltpu.VMEM((slots, wide // 2), F32),
            pltpu.VMEM((slots, wide // 2), F32),
        ],
        compiler_params=params("arbitrary"),
        name="expert",
    )(x, g, weights)


def combine_kernel(back_ref, gate_ref, mix_ref, own_ref, tokens_ref, gates_ref):
    half = pl.program_id(0) % 2
    total = dot(mix_ref[half, 0], back_ref[...]) + dot(mix_ref[half, 1], back_ref[...])
    tokens_ref[...] = total.astype(BF16)

    @pl.when(pl.program_id(0) == 0)
    def _():
        column = gate_ref[:, 0:1].astype(F32)
        for choice in range(2):
            picked = jnp.sum(own_ref[choice].astype(F32) * column, axis=0, keepdims=True)
            gates_ref[choice : choice + 1, :] = picked.astype(BF16)


def combine(back, mix, own):
    total, wide = back.shape
    count = mix.shape[2]
    half_width = wide - 128
    blocks = 4
    block = half_width // blocks
    whole = lambda shape: pl.BlockSpec(shape, lambda i: (0,) * len(shape))
    return pl.pallas_call(
        combine_kernel,
        grid=(2 * blocks,),
        in_specs=[
            pl.BlockSpec((total, block), lambda i: (0, i // 2)),
            pl.BlockSpec((total, 128), lambda i: (0, half_width // 128)),
            whole(mix.shape),
            whole(own.shape),
        ],
        out_specs=[
            pl.BlockSpec((count, block), lambda i: (0, (i % 2) * blocks + i // 2)),
            whole((2, count)),
        ],
        out_shape=[
            jax.ShapeDtypeStruct((count, 2 * half_width), BF16),
            jax.ShapeDtypeStruct((2, count), BF16),
        ],
        compiler_params=params("arbitrary"),
        name="combine",
    )(back, back, mix, own)


def body(tokens, expert_ids, gate_probs, up_weight, down_weight, out_grad):
    experts = lax.axis_size("expert")
    count, width = tokens.shape
    capacity = 3 * count // (2 * experts)
    shard = jnp.concatenate([up_weight[0], down_weight[0].T], axis=1)
    weights = lax.all_gather(shard, "fsdp", axis=0, tiled=True)
    send, mix, own = dispatch(expert_ids.T, gate_probs.T, tokens, out_grad, experts, capacity)
    recv = lax.all_to_all(send, "expert", split_axis=0, concat_axis=0, tiled=True)
    x, g = unpack(recv.reshape(4 * experts * capacity, width // 2), capacity)
    packed = expert(x, g, weights, capacity)
    back = lax.all_to_all(
        packed.reshape(experts, 2 * capacity, width // 2 + 128),
        "expert",
        split_axis=0,
        concat_axis=0,
        tiled=True,
    )
    d_tokens, d_gates = combine(back.reshape(packed.shape), mix, own)
    return d_tokens, d_gates.T


def solution(mesh):
    placed = (
        P(("fsdp", "expert"), None),
        P(("fsdp", "expert"), None),
        P(("fsdp", "expert"), None),
        P("expert", "fsdp", None),
        P("expert", None, "fsdp"),
        P(("fsdp", "expert"), None),
    )
    return jax.shard_map(
        body,
        mesh=mesh,
        in_specs=placed,
        out_specs=(P(("fsdp", "expert"), None), P(("fsdp", "expert"), None)),
        check_vma=False,
    )
```

```python
import functools

import jax
import jax.numpy as jnp
from jax import lax
from jax.experimental import pallas as pl
from jax.experimental.pallas import tpu as pltpu
from jax.sharding import PartitionSpec as P

F32, BF16 = jnp.float32, jnp.bfloat16
VMEM_LIMIT = 56 * 1024 * 1024


def dot(left, right):
    return jnp.dot(left, right, preferred_element_type=F32)


def dot_t(left, right):
    return lax.dot_general(left, right, (((1,), (1,)), ((), ())), preferred_element_type=F32)


def iota(shape, axis):
    return lax.broadcasted_iota(jnp.int32, shape, axis)


def params(*semantics):
    return pltpu.CompilerParams(dimension_semantics=semantics, vmem_limit_bytes=VMEM_LIMIT)


def slot_table(ids, experts, capacity):
    tokens = ids.shape[1]
    expert = iota((experts, tokens), 0)
    named = (expert == ids[0:1, :]) | (expert == ids[1:2, :])
    before = (iota((tokens, tokens), 0) < iota((tokens, tokens), 1)).astype(F32).astype(BF16)
    count = dot(named.astype(F32).astype(BF16), before)
    return jnp.where(named & (count < capacity), count, -1.0)


def dispatch_kernel(experts, capacity, ids_ref, gates_ref, tl, th, gl, gh, send_ref, mix_ref, own_ref, pick):
    rows = 2 * capacity
    tokens = ids_ref.shape[1]

    @pl.when(pl.program_id(0) == 0)
    def _():
        ids = ids_ref[...]
        table = slot_table(ids, experts, capacity)
        count = experts * rows
        spread = (iota((count, experts), 0) // rows == iota((count, experts), 1)).astype(F32).astype(BF16)
        place = iota((count, tokens), 0) % rows
        slot = dot(spread, table.astype(BF16)).astype(jnp.int32)
        low = slot == place
        high = (slot >= 0) & (slot + capacity == place)
        pick[0] = low.astype(F32).astype(BF16)
        pick[1] = high.astype(F32).astype(BF16)
        expert = iota((experts, tokens), 0)
        gates = gates_ref[...]
        weight = jnp.where(expert == ids[0:1, :], gates[0:1, :], gates[1:2, :])
        coarse = weight.astype(BF16)
        fine = (weight - coarse.astype(F32)).astype(BF16)
        for part, value in enumerate((coarse, fine)):
            wide = dot(spread, value)
            for half, chosen in enumerate((low, high)):
                mix_ref[half, part] = jnp.where(chosen, wide, 0.0).T.astype(BF16)
        whose = iota((count, tokens), 0) // rows
        for choice in range(2):
            own_ref[choice] = (low & (whose == ids[choice : choice + 1, :])).astype(F32).astype(BF16)

    count = experts * rows
    width = send_ref.shape[2]
    for part, (left, right) in enumerate(((tl, th), (gl, gh))):
        moved = dot(pick[0], left[...]) + dot(pick[1], right[...])
        send_ref[:, part * rows : (part + 1) * rows, :] = moved.astype(BF16).reshape(experts, rows, width)


def dispatch(ids, gates, tokens, grads, experts, capacity):
    count, width = tokens.shape
    rows = 2 * capacity
    blocks, block = 4, width // 8
    low = pl.BlockSpec((count, block), lambda i: (0, i))
    high = pl.BlockSpec((count, block), lambda i: (0, i + blocks))
    whole = lambda shape: pl.BlockSpec(shape, lambda i: (0,) * len(shape))
    return pl.pallas_call(
        functools.partial(dispatch_kernel, experts, capacity),
        grid=(blocks,),
        in_specs=[whole(ids.shape), whole(gates.shape), low, high, low, high],
        out_specs=[
            pl.BlockSpec((experts, 2 * rows, block), lambda i: (0, 0, i)),
            whole((2, 2, count, experts * rows)),
            whole((2, experts * rows, count)),
        ],
        out_shape=[
            jax.ShapeDtypeStruct((experts, 2 * rows, width // 2), BF16),
            jax.ShapeDtypeStruct((2, 2, count, experts * rows), BF16),
            jax.ShapeDtypeStruct((2, experts * rows, count), BF16),
        ],
        scratch_shapes=[pltpu.VMEM((2, experts * rows, count), BF16)],
        compiler_params=params("arbitrary"),
        name="dispatch",
    )(ids, gates, tokens, tokens, grads, grads)


IN_VMEM = pl.BlockSpec(memory_space=pltpu.VMEM)
IN_HBM = pl.BlockSpec(memory_space=pltpu.HBM)


def unpack_kernel(capacity, recv_ref, tokens_ref, grads_ref):
    slots, width = tokens_ref.shape
    total, half = recv_ref.shape
    row, column = iota((slots, total), 0), iota((slots, total), 1)
    base = (row // capacity) * (4 * capacity) + row % capacity
    block = half // 4
    for part, out in enumerate((tokens_ref, grads_ref)):
        for side in range(2):
            take = (column == base + (2 * part + side) * capacity).astype(F32).astype(BF16)
            for i in range(4):
                start = side * half + i * block
                moved = dot(take, recv_ref[:, i * block : (i + 1) * block])
                out[:, start : start + block] = moved.astype(BF16)


def unpack(recv, capacity):
    total, half = recv.shape
    return pl.pallas_call(
        functools.partial(unpack_kernel, capacity),
        in_specs=[IN_VMEM],
        out_specs=[IN_VMEM, IN_VMEM],
        out_shape=[jax.ShapeDtypeStruct((total // 4, 2 * half), BF16)] * 2,
        compiler_params=pltpu.CompilerParams(vmem_limit_bytes=16 * 1024 * 1024),
        name="unpack",
    )(recv)


def expert_kernel(capacity, cuts, x_ref, g_ref, w_hbm, out_ref, w, arrived):
    slots, width = x_ref.shape
    wide = w.shape[1] // 2
    loads = []
    for i in range(len(cuts) - 1):
        part = pl.ds(cuts[i], cuts[i + 1] - cuts[i])
        loads.append(pltpu.make_async_copy(w_hbm.at[part], w.at[part], arrived.at[i]))
        loads[i].start()
    rows = 2 * capacity
    row, column = iota((2 * slots, slots), 0), iota((2 * slots, slots), 1)
    base = (row // rows) * capacity + row % rows
    low = (column == base) & (row % rows < capacity)
    high = (column == base - capacity) & (row % rows >= capacity)
    low, high = low.astype(F32).astype(BF16), high.astype(F32).astype(BF16)
    h = a = None
    for i in range(len(cuts) - 1):
        loads[i].wait()
        part = slice(cuts[i], cuts[i + 1])
        more_h, more_a = dot(x_ref[:, part], w[part, :wide]), dot(g_ref[:, part], w[part, wide:])
        h, a = (more_h, more_a) if h is None else (h + more_h, a + more_a)
    cdf = 0.5 * (1.0 + lax.erf(h * 0.7071067811865476))
    density = jnp.exp(-0.5 * h * h) * 0.3989422804014327
    active = (h * cdf).astype(BF16).astype(F32)
    gate = jnp.sum(active * a, axis=1, keepdims=True).astype(BF16)
    hidden_grad = (a * (cdf + h * density)).astype(BF16)
    half = width // 2
    block = half // 4
    for i in range(4):
        left = dot_t(hidden_grad, w[i * block : (i + 1) * block, :wide]).astype(BF16)
        right = dot_t(hidden_grad, w[half + i * block : half + (i + 1) * block, :wide]).astype(BF16)
        out_ref[:, i * block : (i + 1) * block] = (dot(low, left) + dot(high, right)).astype(BF16)
    out_ref[:, half:] = dot(low, jnp.broadcast_to(gate, (slots, 128))).astype(BF16)


def expert(x, g, weights, capacity):
    slots, width = x.shape
    cuts = tuple(width * eighth // 8 for eighth in (0, 1, 2, 4, 6, 8))
    return pl.pallas_call(
        functools.partial(expert_kernel, capacity, cuts),
        in_specs=[IN_VMEM, IN_VMEM, IN_HBM],
        out_specs=IN_VMEM,
        out_shape=jax.ShapeDtypeStruct((2 * slots, width // 2 + 128), BF16),
        scratch_shapes=[
            pltpu.VMEM(weights.shape, BF16),
            pltpu.SemaphoreType.DMA((len(cuts) - 1,)),
        ],
        compiler_params=pltpu.CompilerParams(vmem_limit_bytes=40 * 1024 * 1024),
        name="expert",
    )(x, g, weights)


def combine_kernel(blocks, back_ref, mix_ref, own_ref, tokens_hbm, gates_ref, out, left):
    count, width = out.shape
    half = width // 2
    block = half // blocks
    stores = []
    for i in range(blocks):
        total = dot(mix_ref[...], back_ref[:, i * block : (i + 1) * block])
        for side in range(2):
            coarse, fine = (total[(2 * side + j) * count : (2 * side + j + 1) * count] for j in range(2))
            start = side * half + i * block
            out[:, start : start + block] = (coarse + fine).astype(BF16)
            part = pl.ds(start, block)
            stores.append(pltpu.make_async_copy(out.at[:, part], tokens_hbm.at[:, part], left.at[2 * i + side]))
            stores[-1].start()
    column = back_ref[:, half : half + 1].astype(F32)
    for choice in range(2):
        picked = jnp.sum(own_ref[choice].astype(F32) * column, axis=0, keepdims=True)
        gates_ref[choice : choice + 1, :] = picked.astype(BF16)
    for store in stores:
        store.wait()


def combine(back, mix, own):
    half = back.shape[1] - 128
    count = own.shape[2]
    blocks = 4
    return pl.pallas_call(
        functools.partial(combine_kernel, blocks),
        in_specs=[IN_VMEM, IN_VMEM, IN_VMEM],
        out_specs=[IN_HBM, IN_VMEM],
        out_shape=[
            jax.ShapeDtypeStruct((count, 2 * half), BF16),
            jax.ShapeDtypeStruct((2, count), BF16),
        ],
        scratch_shapes=[
            pltpu.VMEM((count, 2 * half), BF16),
            pltpu.SemaphoreType.DMA((2 * blocks,)),
        ],
        compiler_params=pltpu.CompilerParams(vmem_limit_bytes=16 * 1024 * 1024),
        name="combine",
    )(back, mix, own)


def join_kernel(up_ref, down_ref, out_ref):
    width = up_ref.shape[2]
    out_ref[:, :width] = up_ref[0]
    out_ref[:, width:] = down_ref[0].T


def join(up, down):
    return pl.pallas_call(
        join_kernel,
        in_specs=[IN_VMEM, IN_VMEM],
        out_specs=IN_VMEM,
        out_shape=jax.ShapeDtypeStruct((up.shape[1], 2 * up.shape[2]), BF16),
        name="join",
    )(up, down)


def body(tokens, expert_ids, gate_probs, up_weight, down_weight, out_grad):
    experts = lax.axis_size("expert")
    count, width = tokens.shape
    capacity = 3 * count // (2 * experts)
    weights = lax.all_gather(join(up_weight, down_weight), "fsdp", axis=0, tiled=True)
    send, mix, own = dispatch(expert_ids.T, gate_probs.T, tokens, out_grad, experts, capacity)
    recv = lax.all_to_all(send, "expert", split_axis=0, concat_axis=0, tiled=True)
    x, g = unpack(recv.reshape(4 * experts * capacity, width // 2), capacity)
    packed = expert(x, g, weights, capacity)
    back = lax.all_to_all(
        packed.reshape(experts, 2 * capacity, width // 2 + 128),
        "expert",
        split_axis=0,
        concat_axis=0,
        tiled=True,
    )
    d_tokens, d_gates = combine(back.reshape(packed.shape), mix.reshape(4 * count, -1), own)
    return d_tokens, d_gates.T


def solution(mesh):
    placed = (
        P(("fsdp", "expert"), None),
        P(("fsdp", "expert"), None),
        P(("fsdp", "expert"), None),
        P("expert", "fsdp", None),
        P("expert", None, "fsdp"),
        P(("fsdp", "expert"), None),
    )
    return jax.shard_map(
        body,
        mesh=mesh,
        in_specs=placed,
        out_specs=(P(("fsdp", "expert"), None), P(("fsdp", "expert"), None)),
        check_vma=False,
    )
```

```python
import functools
import math

import jax
import jax.numpy as jnp
from jax import lax
from jax.experimental import pallas as pl
from jax.experimental.pallas import tpu as pltpu
from jax.sharding import PartitionSpec as P

F32, BF16 = jnp.float32, jnp.bfloat16
VMEM_LIMIT = 56 * 1024 * 1024


def dot(left, right):
    return jnp.dot(left, right, preferred_element_type=F32)


def dot_t(left, right):
    return lax.dot_general(left, right, (((1,), (1,)), ((), ())), preferred_element_type=F32)


def iota(shape, axis):
    return lax.broadcasted_iota(jnp.int32, shape, axis)


def params(*semantics):
    return pltpu.CompilerParams(dimension_semantics=semantics, vmem_limit_bytes=VMEM_LIMIT)


def slot_table(ids, experts, capacity):
    tokens = ids.shape[1]
    expert = iota((experts, tokens), 0)
    named = (expert == ids[0:1, :]) | (expert == ids[1:2, :])
    before = (iota((tokens, tokens), 0) < iota((tokens, tokens), 1)).astype(F32).astype(BF16)
    count = dot(named.astype(F32).astype(BF16), before)
    return jnp.where(named & (count < capacity), count, -1.0)


def dispatch_kernel(experts, capacity, ids_ref, gates_ref, tl, th, gl, gh, send_ref, mix_ref, own_ref, pick):
    rows = 2 * capacity
    tokens = ids_ref.shape[1]

    @pl.when(pl.program_id(0) == 0)
    def _():
        ids = ids_ref[...]
        table = slot_table(ids, experts, capacity)
        count = experts * rows
        spread = (iota((count, experts), 0) // rows == iota((count, experts), 1)).astype(F32).astype(BF16)
        place = iota((count, tokens), 0) % rows
        slot = dot(spread, table.astype(BF16)).astype(jnp.int32)
        low = slot == place
        high = (slot >= 0) & (slot + capacity == place)
        pick[0] = low.astype(F32).astype(BF16)
        pick[1] = high.astype(F32).astype(BF16)
        expert = iota((experts, tokens), 0)
        gates = gates_ref[...]
        weight = jnp.where(expert == ids[0:1, :], gates[0:1, :], gates[1:2, :])
        coarse = weight.astype(BF16)
        fine = (weight - coarse.astype(F32)).astype(BF16)
        for part, value in enumerate((coarse, fine)):
            wide = dot(spread, value)
            for half, chosen in enumerate((low, high)):
                mix_ref[half, part] = jnp.where(chosen, wide, 0.0).T.astype(BF16)
        whose = iota((count, tokens), 0) // rows
        for choice in range(2):
            own_ref[choice] = (low & (whose == ids[choice : choice + 1, :])).astype(F32).astype(BF16)

    count = experts * rows
    width = send_ref.shape[2]
    for part, (left, right) in enumerate(((tl, th), (gl, gh))):
        moved = dot(pick[0], left[...]) + dot(pick[1], right[...])
        send_ref[:, part * rows : (part + 1) * rows, :] = moved.astype(BF16).reshape(experts, rows, width)


def dispatch(ids, gates, tokens, grads, experts, capacity):
    count, width = tokens.shape
    rows = 2 * capacity
    blocks, block = 4, width // 8
    low = pl.BlockSpec((count, block), lambda i: (0, i))
    high = pl.BlockSpec((count, block), lambda i: (0, i + blocks))
    whole = lambda shape: pl.BlockSpec(shape, lambda i: (0,) * len(shape))
    return pl.pallas_call(
        functools.partial(dispatch_kernel, experts, capacity),
        grid=(blocks,),
        in_specs=[whole(ids.shape), whole(gates.shape), low, high, low, high],
        out_specs=[
            pl.BlockSpec((experts, 2 * rows, block), lambda i: (0, 0, i)),
            whole((2, 2, count, experts * rows)),
            whole((2, experts * rows, count)),
        ],
        out_shape=[
            jax.ShapeDtypeStruct((experts, 2 * rows, width // 2), BF16),
            jax.ShapeDtypeStruct((2, 2, count, experts * rows), BF16),
            jax.ShapeDtypeStruct((2, experts * rows, count), BF16),
        ],
        scratch_shapes=[pltpu.VMEM((2, experts * rows, count), BF16)],
        compiler_params=params("arbitrary"),
        name="dispatch",
    )(ids, gates, tokens, tokens, grads, grads)


IN_VMEM = pl.BlockSpec(memory_space=pltpu.VMEM)
IN_HBM = pl.BlockSpec(memory_space=pltpu.HBM)


def unpack_kernel(capacity, recv_ref, tokens_ref, grads_ref):
    slots, width = tokens_ref.shape
    total, half = recv_ref.shape
    row, column = iota((slots, total), 0), iota((slots, total), 1)
    base = (row // capacity) * (4 * capacity) + row % capacity
    block = half // 4
    for part, out in enumerate((tokens_ref, grads_ref)):
        for side in range(2):
            take = (column == base + (2 * part + side) * capacity).astype(F32).astype(BF16)
            for i in range(4):
                start = side * half + i * block
                moved = dot(take, recv_ref[:, i * block : (i + 1) * block])
                out[:, start : start + block] = moved.astype(BF16)


def unpack(recv, capacity):
    total, half = recv.shape
    return pl.pallas_call(
        functools.partial(unpack_kernel, capacity),
        in_specs=[IN_VMEM],
        out_specs=[IN_VMEM, IN_VMEM],
        out_shape=[jax.ShapeDtypeStruct((total // 4, 2 * half), BF16)] * 2,
        compiler_params=pltpu.CompilerParams(vmem_limit_bytes=16 * 1024 * 1024),
        name="unpack",
    )(recv)


def expert_kernel(capacity, cuts, x_ref, g_ref, w_hbm, out_ref, w, arrived):
    slots, width = x_ref.shape
    wide = w.shape[1] // 2
    loads = []
    for i in range(len(cuts) - 1):
        part = pl.ds(cuts[i], cuts[i + 1] - cuts[i])
        loads.append(pltpu.make_async_copy(w_hbm.at[part], w.at[part], arrived.at[i]))
        loads[i].start()
    rows = 2 * capacity
    row, column = iota((2 * slots, slots), 0), iota((2 * slots, slots), 1)
    base = (row // rows) * capacity + row % rows
    low = (column == base) & (row % rows < capacity)
    high = (column == base - capacity) & (row % rows >= capacity)
    low, high = low.astype(F32).astype(BF16), high.astype(F32).astype(BF16)
    h = a = None
    for i in range(len(cuts) - 1):
        loads[i].wait()
        part = slice(cuts[i], cuts[i + 1])
        more_h, more_a = dot(x_ref[:, part], w[part, :wide]), dot(g_ref[:, part], w[part, wide:])
        h, a = (more_h, more_a) if h is None else (h + more_h, a + more_a)
    cdf = 0.5 * (1.0 + lax.erf(h * 0.7071067811865476))
    density = jnp.exp(-0.5 * h * h) * 0.3989422804014327
    active = (h * cdf).astype(BF16).astype(F32)
    gate = jnp.sum(active * a, axis=1, keepdims=True).astype(BF16)
    hidden_grad = (a * (cdf + h * density)).astype(BF16)
    half = width // 2
    block = half // 4
    for i in range(4):
        left = dot_t(hidden_grad, w[i * block : (i + 1) * block, :wide]).astype(BF16)
        right = dot_t(hidden_grad, w[half + i * block : half + (i + 1) * block, :wide]).astype(BF16)
        out_ref[:, i * block : (i + 1) * block] = (dot(low, left) + dot(high, right)).astype(BF16)
    out_ref[:, half:] = dot(low, jnp.broadcast_to(gate, (slots, 128))).astype(BF16)


def expert(x, g, weights, capacity):
    slots, width = x.shape
    cuts = tuple(width * eighth // 8 for eighth in (0, 1, 2, 4, 6, 8))
    return pl.pallas_call(
        functools.partial(expert_kernel, capacity, cuts),
        in_specs=[IN_VMEM, IN_VMEM, IN_HBM],
        out_specs=IN_VMEM,
        out_shape=jax.ShapeDtypeStruct((2 * slots, width // 2 + 128), BF16),
        scratch_shapes=[
            pltpu.VMEM(weights.shape, BF16),
            pltpu.SemaphoreType.DMA((len(cuts) - 1,)),
        ],
        compiler_params=pltpu.CompilerParams(vmem_limit_bytes=40 * 1024 * 1024),
        name="expert",
    )(x, g, weights)


def combine_kernel(blocks, back_ref, mix_ref, own_ref, tokens_hbm, gates_ref, out, left):
    count, width = out.shape
    half = width // 2
    block = half // blocks
    stores = []
    for i in range(blocks):
        total = dot(mix_ref[...], back_ref[:, i * block : (i + 1) * block])
        for side in range(2):
            coarse, fine = (total[(2 * side + j) * count : (2 * side + j + 1) * count] for j in range(2))
            start = side * half + i * block
            out[:, start : start + block] = (coarse + fine).astype(BF16)
            part = pl.ds(start, block)
            stores.append(pltpu.make_async_copy(out.at[:, part], tokens_hbm.at[:, part], left.at[2 * i + side]))
            stores[-1].start()
    column = back_ref[:, half : half + 1].astype(F32)
    for choice in range(2):
        picked = jnp.sum(own_ref[choice].astype(F32) * column, axis=0, keepdims=True)
        gates_ref[choice : choice + 1, :] = picked.astype(BF16)
    for store in stores:
        store.wait()


def combine(back, mix, own):
    half = back.shape[1] - 128
    count = own.shape[2]
    blocks = 4
    return pl.pallas_call(
        functools.partial(combine_kernel, blocks),
        in_specs=[IN_VMEM, IN_VMEM, IN_VMEM],
        out_specs=[IN_HBM, IN_VMEM],
        out_shape=[
            jax.ShapeDtypeStruct((count, 2 * half), BF16),
            jax.ShapeDtypeStruct((2, count), BF16),
        ],
        scratch_shapes=[
            pltpu.VMEM((count, 2 * half), BF16),
            pltpu.SemaphoreType.DMA((2 * blocks,)),
        ],
        compiler_params=pltpu.CompilerParams(vmem_limit_bytes=16 * 1024 * 1024),
        name="combine",
    )(back, mix, own)


def join_kernel(up_ref, down_ref, out_ref):
    width = up_ref.shape[2]
    out_ref[:, :width] = up_ref[0]
    out_ref[:, width:] = down_ref[0].T


def join(up, down):
    return pl.pallas_call(
        join_kernel,
        in_specs=[IN_VMEM, IN_VMEM],
        out_specs=IN_VMEM,
        out_shape=jax.ShapeDtypeStruct((up.shape[1], 2 * up.shape[2]), BF16),
        name="join",
    )(up, down)


def exchange_orders(side):
    first = [((i % side + i // side) % side) * side + i % side for i in range(side * side)]
    return first, [(device % side) * side + device // side for device in first]


def place_in_order(ids, side, core):
    x, y = ids // side, ids % side
    along, across = jnp.where(core == 0, x, y), jnp.where(core == 0, y, x)
    return ((along - across) % side) * side + across


def body(tokens, expert_ids, gate_probs, up_weight, down_weight, out_grad):
    experts = lax.axis_size("expert")
    planes = lax.axis_size("fsdp")
    side = math.isqrt(experts)
    orders = exchange_orders(side)
    groups = [[plane * experts + device for device in orders[plane % 2]] for plane in range(planes)]
    exchange = functools.partial(
        lax.all_to_all,
        axis_name=("fsdp", "expert"),
        split_axis=0,
        concat_axis=0,
        tiled=True,
        axis_index_groups=groups,
    )
    count, width = tokens.shape
    capacity = 3 * count // (2 * experts)
    weights = lax.all_gather(join(up_weight, down_weight), "fsdp", axis=0, tiled=True)
    places = place_in_order(expert_ids.T, side, lax.axis_index("fsdp") % 2)
    send, mix, own = dispatch(places, gate_probs.T, tokens, out_grad, experts, capacity)
    recv = exchange(send)
    x, g = unpack(recv.reshape(4 * experts * capacity, width // 2), capacity)
    packed = expert(x, g, weights, capacity)
    back = exchange(packed.reshape(experts, 2 * capacity, width // 2 + 128))
    d_tokens, d_gates = combine(back.reshape(packed.shape), mix.reshape(4 * count, -1), own)
    return d_tokens, d_gates.T


def solution(mesh):
    placed = (
        P(("fsdp", "expert"), None),
        P(("fsdp", "expert"), None),
        P(("fsdp", "expert"), None),
        P("expert", "fsdp", None),
        P("expert", None, "fsdp"),
        P(("fsdp", "expert"), None),
    )
    return jax.shard_map(
        body,
        mesh=mesh,
        in_specs=placed,
        out_specs=(P(("fsdp", "expert"), None), P(("fsdp", "expert"), None)),
        check_vma=False,
    )
```

```python
import functools
import math

import jax
import jax.numpy as jnp
from jax import lax
from jax.experimental import pallas as pl
from jax.experimental.pallas import tpu as pltpu
from jax.sharding import PartitionSpec as P

F32, BF16 = jnp.float32, jnp.bfloat16
VMEM_LIMIT = 56 * 1024 * 1024
HEAD = 8


def dot(left, right):
    return jnp.dot(left, right, preferred_element_type=F32)


def dot_t(left, right):
    return lax.dot_general(left, right, (((1,), (1,)), ((), ())), preferred_element_type=F32)


def iota(shape, axis):
    return lax.broadcasted_iota(jnp.int32, shape, axis)


def params(*semantics):
    return pltpu.CompilerParams(dimension_semantics=semantics, vmem_limit_bytes=VMEM_LIMIT)


def slot_table(ids, experts, capacity):
    tokens = ids.shape[1]
    expert = iota((experts, tokens), 0)
    named = (expert == ids[0:1, :]) | (expert == ids[1:2, :])
    before = (iota((tokens, tokens), 0) < iota((tokens, tokens), 1)).astype(F32).astype(BF16)
    count = dot(named.astype(F32).astype(BF16), before)
    return jnp.where(named & (count < capacity), count, -1.0)


def dispatch_kernel(experts, capacity, ids_ref, gates_ref, tl, th, gl, gh, send_ref, mix_ref, own_ref, pick):
    rows = 2 * capacity
    tokens = ids_ref.shape[1]

    @pl.when(pl.program_id(0) == 0)
    def _():
        ids = ids_ref[...]
        table = slot_table(ids, experts, capacity)
        count = experts * rows
        spread = (iota((count, experts), 0) // rows == iota((count, experts), 1)).astype(F32).astype(BF16)
        place = iota((count, tokens), 0) % rows
        slot = dot(spread, table.astype(BF16)).astype(jnp.int32)
        low = slot == place
        high = (slot >= 0) & (slot + capacity == place)
        pick[0] = low.astype(F32).astype(BF16)
        pick[1] = high.astype(F32).astype(BF16)
        expert = iota((experts, tokens), 0)
        gates = gates_ref[...]
        weight = jnp.where(expert == ids[0:1, :], gates[0:1, :], gates[1:2, :])
        coarse = weight.astype(BF16)
        fine = (weight - coarse.astype(F32)).astype(BF16)
        short = experts * HEAD
        tail = capacity - HEAD
        spread = (iota((short, experts), 0) // HEAD == iota((short, experts), 1)).astype(F32).astype(BF16)
        place = iota((short, tokens), 0) % HEAD
        slot = dot(spread, table.astype(BF16)).astype(jnp.int32)
        whole = slot == place
        sides = ((place < tail) & (slot == HEAD + place), (place >= tail) & (slot == HEAD + place - tail))
        for part, value in enumerate((coarse, fine)):
            wide = dot(spread, value)
            lines = slice(part * tokens, (part + 1) * tokens)
            for half, chosen in enumerate(sides):
                mix_ref[half, lines, :short] = jnp.where(whole, wide, 0.0).T.astype(BF16)
                mix_ref[half, lines, short:] = jnp.where(chosen, wide, 0.0).T.astype(BF16)
        whose = iota((short, tokens), 0) // HEAD
        for choice in range(2):
            mine = whose == ids[choice : choice + 1, :]
            own_ref[choice, :short] = (whole & mine).astype(F32).astype(BF16)
            own_ref[choice, short:] = (sides[0] & mine).astype(F32).astype(BF16)

    count = experts * rows
    width = send_ref.shape[2]
    for part, (left, right) in enumerate(((tl, th), (gl, gh))):
        moved = dot(pick[0], left[...]) + dot(pick[1], right[...])
        send_ref[:, part * rows : (part + 1) * rows, :] = moved.astype(BF16).reshape(experts, rows, width)


def dispatch(ids, gates, tokens, grads, experts, capacity):
    count, width = tokens.shape
    rows = 2 * capacity
    blocks, block = 4, width // 8
    low = pl.BlockSpec((count, block), lambda i: (0, i))
    high = pl.BlockSpec((count, block), lambda i: (0, i + blocks))
    whole = lambda shape: pl.BlockSpec(shape, lambda i: (0,) * len(shape))
    return pl.pallas_call(
        functools.partial(dispatch_kernel, experts, capacity),
        grid=(blocks,),
        in_specs=[whole(ids.shape), whole(gates.shape), low, high, low, high],
        out_specs=[
            pl.BlockSpec((experts, 2 * rows, block), lambda i: (0, 0, i)),
            whole((2, 2 * count, 2 * experts * HEAD)),
            whole((2, 2 * experts * HEAD, count)),
        ],
        out_shape=[
            jax.ShapeDtypeStruct((experts, 2 * rows, width // 2), BF16),
            jax.ShapeDtypeStruct((2, 2 * count, 2 * experts * HEAD), BF16),
            jax.ShapeDtypeStruct((2, 2 * experts * HEAD, count), BF16),
        ],
        scratch_shapes=[pltpu.VMEM((2, experts * rows, count), BF16)],
        compiler_params=params("arbitrary"),
        name="dispatch",
    )(ids, gates, tokens, tokens, grads, grads)


IN_VMEM = pl.BlockSpec(memory_space=pltpu.VMEM)
IN_HBM = pl.BlockSpec(memory_space=pltpu.HBM)


def unpack_kernel(capacity, recv_ref, tokens_ref, grads_ref):
    slots, width = tokens_ref.shape
    total, half = recv_ref.shape
    row, column = iota((slots, total), 0), iota((slots, total), 1)
    tail = capacity - HEAD
    first = HEAD * slots // capacity
    source = jnp.where(row < first, row // HEAD, (row - first) // tail)
    slot = jnp.where(row < first, row % HEAD, HEAD + (row - first) % tail)
    base = source * (4 * capacity) + slot
    block = half // 4
    for part, out in enumerate((tokens_ref, grads_ref)):
        for side in range(2):
            take = (column == base + (2 * part + side) * capacity).astype(F32).astype(BF16)
            for i in range(4):
                start = side * half + i * block
                moved = dot(take, recv_ref[:, i * block : (i + 1) * block])
                out[:, start : start + block] = moved.astype(BF16)


def unpack(recv, capacity):
    total, half = recv.shape
    return pl.pallas_call(
        functools.partial(unpack_kernel, capacity),
        in_specs=[IN_VMEM],
        out_specs=[IN_VMEM, IN_VMEM],
        out_shape=[jax.ShapeDtypeStruct((total // 4, 2 * half), BF16)] * 2,
        compiler_params=pltpu.CompilerParams(vmem_limit_bytes=16 * 1024 * 1024),
        name="unpack",
    )(recv)


def fold(left, right):
    rows, width = left.shape
    left, right = left.reshape(rows // 8, 8, width), right.reshape(rows // 8, 8, width)
    upper = iota(left.shape, 1) < 4
    even = jnp.where(upper, left, pltpu.roll(right, 4, 1))
    odd = jnp.where(upper, pltpu.roll(left, 4, 1), right)
    return jnp.stack([even, odd], axis=1).reshape(2 * rows, width)


def expert_kernel(cuts, x_ref, g_ref, w_hbm, out_ref, w, arrived):
    width = x_ref.shape[1]
    wide = w.shape[1] // 2
    loads = []
    for i in range(len(cuts) - 1):
        part = pl.ds(cuts[i], cuts[i + 1] - cuts[i])
        loads.append(pltpu.make_async_copy(w_hbm.at[part], w.at[part], arrived.at[i]))
        loads[i].start()
    h = a = None
    for i in range(len(cuts) - 1):
        loads[i].wait()
        part = slice(cuts[i], cuts[i + 1])
        more_h, more_a = dot(x_ref[:, part], w[part, :wide]), dot(g_ref[:, part], w[part, wide:])
        h, a = (more_h, more_a) if h is None else (h + more_h, a + more_a)
    cdf = 0.5 * (1.0 + lax.erf(h * 0.7071067811865476))
    density = jnp.exp(-0.5 * h * h) * 0.3989422804014327
    active = (h * cdf).astype(BF16).astype(F32)
    gate = jnp.sum(active * a, axis=1, keepdims=True)
    hidden_grad = (a * (cdf + h * density)).astype(BF16)
    first = out_ref.shape[0]
    half = width // 2
    block = half // 4
    for i in range(4):
        left = dot_t(hidden_grad, w[i * block : (i + 1) * block, :wide])
        right = dot_t(hidden_grad, w[half + i * block : half + (i + 1) * block, :wide])
        out_ref[:, i * block : (i + 1) * block] = left[:first].astype(BF16)
        out_ref[:, half + i * block : half + (i + 1) * block] = right[:first].astype(BF16)
        out_ref[:, width + i * block : width + (i + 1) * block] = fold(left[first:], right[first:]).astype(BF16)
    lanes = jnp.broadcast_to(gate, (gate.shape[0], 128))
    rest = fold(lanes[first:], lanes[first:])
    out_ref[:, width + half :] = jnp.where(iota(rest.shape, 1) < 64, lanes[:first], rest).astype(BF16)


def expert(x, g, weights, capacity):
    slots, width = x.shape
    cuts = tuple(width * eighth // 8 for eighth in (0, 1, 2, 4, 6, 8))
    return pl.pallas_call(
        functools.partial(expert_kernel, cuts),
        in_specs=[IN_VMEM, IN_VMEM, IN_HBM],
        out_specs=IN_VMEM,
        out_shape=jax.ShapeDtypeStruct((HEAD * slots // capacity, 3 * width // 2 + 128), BF16),
        scratch_shapes=[
            pltpu.VMEM(weights.shape, BF16),
            pltpu.SemaphoreType.DMA((len(cuts) - 1,)),
        ],
        compiler_params=pltpu.CompilerParams(vmem_limit_bytes=40 * 1024 * 1024),
        name="expert",
    )(x, g, weights)


def combine_kernel(blocks, back_ref, mix_ref, own_ref, tokens_hbm, gates_ref, out, left):
    count, width = out.shape
    half = width // 2
    block = half // blocks
    stores = []
    for i in range(blocks):
        rest = back_ref[:, width + i * block : width + (i + 1) * block]
        for side in range(2):
            start = side * half + i * block
            rows = jnp.concatenate([back_ref[:, start : start + block], rest], axis=0)
            total = dot(mix_ref[side], rows)
            out[:, start : start + block] = (total[:count] + total[count:]).astype(BF16)
            part = pl.ds(start, block)
            stores.append(pltpu.make_async_copy(out.at[:, part], tokens_hbm.at[:, part], left.at[2 * i + side]))
            stores[-1].start()
    lanes = back_ref[:, width + half :].astype(F32)
    column = jnp.concatenate([lanes[:, 0:1], lanes[:, 64:65]], axis=0)
    for choice in range(2):
        picked = jnp.sum(own_ref[choice].astype(F32) * column, axis=0, keepdims=True)
        gates_ref[choice : choice + 1, :] = picked.astype(BF16)
    for store in stores:
        store.wait()


def combine(back, mix, own, width):
    count = own.shape[2]
    blocks = 4
    return pl.pallas_call(
        functools.partial(combine_kernel, blocks),
        in_specs=[IN_VMEM, IN_VMEM, IN_VMEM],
        out_specs=[IN_HBM, IN_VMEM],
        out_shape=[
            jax.ShapeDtypeStruct((count, width), BF16),
            jax.ShapeDtypeStruct((2, count), BF16),
        ],
        scratch_shapes=[
            pltpu.VMEM((count, width), BF16),
            pltpu.SemaphoreType.DMA((2 * blocks,)),
        ],
        compiler_params=pltpu.CompilerParams(vmem_limit_bytes=16 * 1024 * 1024),
        name="combine",
    )(back, mix, own)


def join_kernel(up_ref, down_ref, out_ref):
    width = up_ref.shape[2]
    out_ref[:, :width] = up_ref[0]
    out_ref[:, width:] = down_ref[0].T


def join(up, down):
    return pl.pallas_call(
        join_kernel,
        in_specs=[IN_VMEM, IN_VMEM],
        out_specs=IN_VMEM,
        out_shape=jax.ShapeDtypeStruct((up.shape[1], 2 * up.shape[2]), BF16),
        name="join",
    )(up, down)


def exchange_orders(side):
    first = [((i % side + i // side) % side) * side + i % side for i in range(side * side)]
    return first, [(device % side) * side + device // side for device in first]


def place_in_order(ids, side, core):
    x, y = ids // side, ids % side
    along, across = jnp.where(core == 0, x, y), jnp.where(core == 0, y, x)
    return ((along - across) % side) * side + across


def body(tokens, expert_ids, gate_probs, up_weight, down_weight, out_grad):
    experts = lax.axis_size("expert")
    planes = lax.axis_size("fsdp")
    side = math.isqrt(experts)
    orders = exchange_orders(side)
    groups = [[plane * experts + device for device in orders[plane % 2]] for plane in range(planes)]
    exchange = functools.partial(
        lax.all_to_all,
        axis_name=("fsdp", "expert"),
        split_axis=0,
        concat_axis=0,
        tiled=True,
        axis_index_groups=groups,
    )
    count, width = tokens.shape
    capacity = 3 * count // (2 * experts)
    weights = lax.all_gather(join(up_weight, down_weight), "fsdp", axis=0, tiled=True)
    places = place_in_order(expert_ids.T, side, lax.axis_index("fsdp") % 2)
    send, mix, own = dispatch(places, gate_probs.T, tokens, out_grad, experts, capacity)
    recv = exchange(send)
    x, g = unpack(recv.reshape(4 * experts * capacity, width // 2), capacity)
    packed = expert(x, g, weights, capacity)
    back = exchange(packed.reshape(experts, HEAD, -1))
    d_tokens, d_gates = combine(back.reshape(packed.shape), mix, own, width)
    return d_tokens, d_gates.T


def solution(mesh):
    placed = (
        P(("fsdp", "expert"), None),
        P(("fsdp", "expert"), None),
        P(("fsdp", "expert"), None),
        P("expert", "fsdp", None),
        P("expert", None, "fsdp"),
        P(("fsdp", "expert"), None),
    )
    return jax.shard_map(
        body,
        mesh=mesh,
        in_specs=placed,
        out_specs=(P(("fsdp", "expert"), None), P(("fsdp", "expert"), None)),
        check_vma=False,
    )
```

```python
import functools
import math

import jax
import jax.numpy as jnp
from jax import lax
from jax.experimental import pallas as pl
from jax.experimental.pallas import tpu as pltpu
from jax.sharding import PartitionSpec as P

F32, BF16 = jnp.float32, jnp.bfloat16
VMEM_LIMIT = 56 * 1024 * 1024
HEAD = 8


def dot(left, right):
    return jnp.dot(left, right, preferred_element_type=F32)


def dot_t(left, right):
    return lax.dot_general(left, right, (((1,), (1,)), ((), ())), preferred_element_type=F32)


def iota(shape, axis):
    return lax.broadcasted_iota(jnp.int32, shape, axis)


def params(*semantics):
    return pltpu.CompilerParams(dimension_semantics=semantics, vmem_limit_bytes=VMEM_LIMIT)


def slot_table(ids, experts, capacity):
    tokens = ids.shape[1]
    expert = iota((experts, tokens), 0)
    named = (expert == ids[0:1, :]) | (expert == ids[1:2, :])
    before = (iota((tokens, tokens), 0) < iota((tokens, tokens), 1)).astype(F32).astype(BF16)
    count = dot(named.astype(F32).astype(BF16), before)
    return jnp.where(named & (count < capacity), count, -1.0)


def dispatch_kernel(experts, capacity, ids_ref, gates_ref, tl, th, gl, gh, send_ref, mix_ref, own_ref, pick):
    rows = 2 * capacity
    tokens = ids_ref.shape[1]

    @pl.when(pl.program_id(0) == 0)
    def _():
        ids = ids_ref[...]
        table = slot_table(ids, experts, capacity)
        count = experts * rows
        spread = (iota((count, experts), 0) // rows == iota((count, experts), 1)).astype(F32).astype(BF16)
        place = iota((count, tokens), 0) % rows
        slot = dot(spread, table.astype(BF16)).astype(jnp.int32)
        low = slot == place
        high = (slot >= 0) & (slot + capacity == place)
        pick[0] = low.astype(F32).astype(BF16)
        pick[1] = high.astype(F32).astype(BF16)
        expert = iota((experts, tokens), 0)
        gates = gates_ref[...]
        weight = jnp.where(expert == ids[0:1, :], gates[0:1, :], gates[1:2, :])
        coarse = weight.astype(BF16)
        fine = (weight - coarse.astype(F32)).astype(BF16)
        short = experts * HEAD
        tail = capacity - HEAD
        spread = (iota((short, experts), 0) // HEAD == iota((short, experts), 1)).astype(F32).astype(BF16)
        place = iota((short, tokens), 0) % HEAD
        slot = dot(spread, table.astype(BF16)).astype(jnp.int32)
        whole = slot == place
        sides = ((place < tail) & (slot == HEAD + place), (place >= tail) & (slot == HEAD + place - tail))
        for part, value in enumerate((coarse, fine)):
            wide = dot(spread, value)
            lines = slice(part * tokens, (part + 1) * tokens)
            for half, chosen in enumerate(sides):
                mix_ref[half, lines, :short] = jnp.where(whole, wide, 0.0).T.astype(BF16)
                mix_ref[half, lines, short:] = jnp.where(chosen, wide, 0.0).T.astype(BF16)
        whose = iota((short, tokens), 0) // HEAD
        for choice in range(2):
            mine = whose == ids[choice : choice + 1, :]
            own_ref[choice, :short] = (whole & mine).astype(F32).astype(BF16)
            own_ref[choice, short:] = (sides[0] & mine).astype(F32).astype(BF16)

    count = experts * rows
    width = send_ref.shape[2]
    for part, (left, right) in enumerate(((tl, th), (gl, gh))):
        moved = dot(pick[0], left[...]) + dot(pick[1], right[...])
        send_ref[:, part * rows : (part + 1) * rows, :] = moved.astype(BF16).reshape(experts, rows, width)


def dispatch(ids, gates, tokens, grads, experts, capacity):
    count, width = tokens.shape
    rows = 2 * capacity
    blocks, block = 4, width // 8
    low = pl.BlockSpec((count, block), lambda i: (0, i))
    high = pl.BlockSpec((count, block), lambda i: (0, i + blocks))
    whole = lambda shape: pl.BlockSpec(shape, lambda i: (0,) * len(shape))
    return pl.pallas_call(
        functools.partial(dispatch_kernel, experts, capacity),
        grid=(blocks,),
        in_specs=[whole(ids.shape), whole(gates.shape), low, high, low, high],
        out_specs=[
            pl.BlockSpec((experts, 2 * rows, block), lambda i: (0, 0, i)),
            whole((2, 2 * count, 2 * experts * HEAD)),
            whole((2, 2 * experts * HEAD, count)),
        ],
        out_shape=[
            jax.ShapeDtypeStruct((experts, 2 * rows, width // 2), BF16),
            jax.ShapeDtypeStruct((2, 2 * count, 2 * experts * HEAD), BF16),
            jax.ShapeDtypeStruct((2, 2 * experts * HEAD, count), BF16),
        ],
        scratch_shapes=[pltpu.VMEM((2, experts * rows, count), BF16)],
        compiler_params=params("arbitrary"),
        name="dispatch",
    )(ids, gates, tokens, tokens, grads, grads)


IN_VMEM = pl.BlockSpec(memory_space=pltpu.VMEM)
IN_HBM = pl.BlockSpec(memory_space=pltpu.HBM)


def unpack_kernel(capacity, recv_ref, tokens_ref, grads_ref):
    slots, width = tokens_ref.shape
    total, half = recv_ref.shape
    row, column = iota((slots, total), 0), iota((slots, total), 1)
    tail = capacity - HEAD
    first = HEAD * slots // capacity
    source = jnp.where(row < first, row // HEAD, (row - first) // tail)
    slot = jnp.where(row < first, row % HEAD, HEAD + (row - first) % tail)
    base = source * (4 * capacity) + slot
    block = half // 4
    for part, out in enumerate((tokens_ref, grads_ref)):
        for side in range(2):
            take = (column == base + (2 * part + side) * capacity).astype(F32).astype(BF16)
            for i in range(4):
                start = side * half + i * block
                moved = dot(take, recv_ref[:, i * block : (i + 1) * block])
                out[:, start : start + block] = moved.astype(BF16)


def unpack(recv, capacity):
    total, half = recv.shape
    return pl.pallas_call(
        functools.partial(unpack_kernel, capacity),
        in_specs=[IN_VMEM],
        out_specs=[IN_VMEM, IN_VMEM],
        out_shape=[jax.ShapeDtypeStruct((total // 4, 2 * half), BF16)] * 2,
        compiler_params=pltpu.CompilerParams(vmem_limit_bytes=16 * 1024 * 1024),
        name="unpack",
    )(recv)


def fold(left, right):
    rows, width = left.shape
    left, right = left.reshape(rows // 8, 8, width), right.reshape(rows // 8, 8, width)
    upper = iota(left.shape, 1) < 4
    even = jnp.where(upper, left, pltpu.roll(right, 4, 1))
    odd = jnp.where(upper, pltpu.roll(left, 4, 1), right)
    return jnp.stack([even, odd], axis=1).reshape(2 * rows, width)


def expert_kernel(cuts, x_ref, g_ref, w_hbm, out_ref, w, arrived):
    width = x_ref.shape[1]
    wide = w.shape[1] // 2
    loads = []
    for i in range(len(cuts) - 1):
        part = pl.ds(cuts[i], cuts[i + 1] - cuts[i])
        loads.append(pltpu.make_async_copy(w_hbm.at[part], w.at[part], arrived.at[i]))
        loads[i].start()
    h = a = None
    for i in range(len(cuts) - 1):
        loads[i].wait()
        part = slice(cuts[i], cuts[i + 1])
        more_h, more_a = dot(x_ref[:, part], w[part, :wide]), dot(g_ref[:, part], w[part, wide:])
        h, a = (more_h, more_a) if h is None else (h + more_h, a + more_a)
    cdf = 0.5 * (1.0 + lax.erf(h * 0.7071067811865476))
    density = jnp.exp(-0.5 * h * h) * 0.3989422804014327
    active = (h * cdf).astype(BF16).astype(F32)
    gate = jnp.sum(active * a, axis=1, keepdims=True)
    hidden_grad = (a * (cdf + h * density)).astype(BF16)
    first = out_ref.shape[0]
    half = width // 2
    block = half // 4
    for i in range(4):
        left = dot_t(hidden_grad, w[i * block : (i + 1) * block, :wide])
        right = dot_t(hidden_grad, w[half + i * block : half + (i + 1) * block, :wide])
        out_ref[:, i * block : (i + 1) * block] = left[:first].astype(BF16)
        out_ref[:, half + i * block : half + (i + 1) * block] = right[:first].astype(BF16)
        out_ref[:, width + i * block : width + (i + 1) * block] = fold(left[first:], right[first:]).astype(BF16)
    lanes = jnp.broadcast_to(gate, (gate.shape[0], 128))
    rest = fold(lanes[first:], lanes[first:])
    out_ref[:, width + half :] = jnp.where(iota(rest.shape, 1) < 64, lanes[:first], rest).astype(BF16)


def expert(x, g, weights, capacity):
    slots, width = x.shape
    cuts = tuple(width * eighth // 8 for eighth in (0, 1, 2, 4, 6, 8))
    return pl.pallas_call(
        functools.partial(expert_kernel, cuts),
        in_specs=[IN_VMEM, IN_VMEM, IN_HBM],
        out_specs=IN_VMEM,
        out_shape=jax.ShapeDtypeStruct((HEAD * slots // capacity, 3 * width // 2 + 128), BF16),
        scratch_shapes=[
            pltpu.VMEM(weights.shape, BF16),
            pltpu.SemaphoreType.DMA((len(cuts) - 1,)),
        ],
        compiler_params=pltpu.CompilerParams(vmem_limit_bytes=40 * 1024 * 1024),
        name="expert",
    )(x, g, weights)


def combine_kernel(blocks, back_ref, mix_ref, own_ref, tokens_hbm, gates_ref, out, left):
    count, width = out.shape
    half = width // 2
    block = half // blocks
    stores = []
    for i in range(blocks):
        rest = back_ref[:, width + i * block : width + (i + 1) * block]
        for side in range(2):
            start = side * half + i * block
            rows = jnp.concatenate([back_ref[:, start : start + block], rest], axis=0)
            total = dot(mix_ref[side], rows)
            out[:, start : start + block] = (total[:count] + total[count:]).astype(BF16)
            part = pl.ds(start, block)
            stores.append(pltpu.make_async_copy(out.at[:, part], tokens_hbm.at[:, part], left.at[2 * i + side]))
            stores[-1].start()
    lanes = back_ref[:, width + half :].astype(F32)
    column = jnp.concatenate([lanes[:, 0:1], lanes[:, 64:65]], axis=0)
    for choice in range(2):
        picked = jnp.sum(own_ref[choice].astype(F32) * column, axis=0, keepdims=True)
        gates_ref[choice : choice + 1, :] = picked.astype(BF16)
    for store in stores:
        store.wait()


def combine(back, mix, own, width):
    count = own.shape[2]
    blocks = 4
    return pl.pallas_call(
        functools.partial(combine_kernel, blocks),
        in_specs=[IN_VMEM, IN_VMEM, IN_VMEM],
        out_specs=[IN_HBM, IN_VMEM],
        out_shape=[
            jax.ShapeDtypeStruct((count, width), BF16),
            jax.ShapeDtypeStruct((2, count), BF16),
        ],
        scratch_shapes=[
            pltpu.VMEM((count, width), BF16),
            pltpu.SemaphoreType.DMA((2 * blocks,)),
        ],
        compiler_params=pltpu.CompilerParams(vmem_limit_bytes=16 * 1024 * 1024),
        name="combine",
    )(back, mix, own)


def join_kernel(up_ref, down_ref, out_ref):
    width = up_ref.shape[2]
    out_ref[:, :width] = up_ref[0]
    out_ref[:, width:] = down_ref[0].T


def join(up, down):
    return pl.pallas_call(
        join_kernel,
        in_specs=[IN_VMEM, IN_VMEM],
        out_specs=IN_VMEM,
        out_shape=jax.ShapeDtypeStruct((up.shape[1], 2 * up.shape[2]), BF16),
        name="join",
    )(up, down)


def exchange_orders(side):
    first = list(range(side * side))
    return first, [(device % side) * side + device // side for device in first]


def place_in_order(ids, side, core):
    return jnp.where(core == 0, ids, (ids % side) * side + ids // side)


def body(tokens, expert_ids, gate_probs, up_weight, down_weight, out_grad):
    experts = lax.axis_size("expert")
    planes = lax.axis_size("fsdp")
    side = math.isqrt(experts)
    orders = exchange_orders(side)
    groups = [[plane * experts + device for device in orders[plane % 2]] for plane in range(planes)]
    exchange = functools.partial(
        lax.all_to_all,
        axis_name=("fsdp", "expert"),
        split_axis=0,
        concat_axis=0,
        tiled=True,
        axis_index_groups=groups,
    )
    count, width = tokens.shape
    capacity = 3 * count // (2 * experts)
    weights = lax.all_gather(join(up_weight, down_weight), "fsdp", axis=0, tiled=True)
    places = place_in_order(expert_ids.T, side, lax.axis_index("fsdp") % 2)
    send, mix, own = dispatch(places, gate_probs.T, tokens, out_grad, experts, capacity)
    recv = exchange(send)
    x, g = unpack(recv.reshape(4 * experts * capacity, width // 2), capacity)
    packed = expert(x, g, weights, capacity)
    back = exchange(packed.reshape(experts, HEAD, -1))
    d_tokens, d_gates = combine(back.reshape(packed.shape), mix, own, width)
    return d_tokens, d_gates.T


def solution(mesh):
    placed = (
        P(("fsdp", "expert"), None),
        P(("fsdp", "expert"), None),
        P(("fsdp", "expert"), None),
        P("expert", "fsdp", None),
        P("expert", None, "fsdp"),
        P(("fsdp", "expert"), None),
    )
    return jax.shard_map(
        body,
        mesh=mesh,
        in_specs=placed,
        out_specs=(P(("fsdp", "expert"), None), P(("fsdp", "expert"), None)),
        check_vma=False,
    )
```
